32 devices in a mesh: lat: 8 (over y, x, core), lon: 4 (over z).
Axes of the slice: x: 2, y: 2, z: 4, core: 2. Of those that a mesh axis runs over, the one named last changes fastest.
Arguments:
- grid_state: bfloat16 [384, 768, 128], P('lat', 'lon'), may hold values from -6 to 6
- upstream: bfloat16 [384, 768, 128], P('lat', 'lon'), may hold values from -6 to 6
- spectral_weight: bfloat16 [128, 384, 2, 128], P('lon', 'lat'), may hold values from -0.375 to 0.375
- up_weight: bfloat16 [128, 512], replicated, may hold values from -0.5 to 0.5
- down_weight: bfloat16 [512, 128], replicated, may hold values from -0.25 to 0.25
Outputs:
- next_state: bfloat16 [384, 768, 128], P('lat', 'lon')
- grad_state: bfloat16 [384, 768, 128], P('lat', 'lon')
- grad_spectral: float32 [128, 384, 2, 128], P('lon', 'lat')
- grad_up: float32 [128, 512], replicated
- grad_down: float32 [512, 128], replicated
The draws below stay inside these ranges and needn't reach their ends.
All inputs are finite; a program needn't handle non-finite values.
Results may differ from the reference program's by a relative error of at most 0.02.
Values may be sent and summed in bfloat16 or wider, within the bound.
A program may use at most 256 MiB of HBM per device.

```python
import jax
import jax.numpy as jnp
import numpy as np
from jax import lax

C = 128
FF = 512
L = 384
NLAT = 384
NLON = 768
M = 384


def level_of(key, extent, shards, low, high):
    loudness, own = 1.0, jax.random.fold_in(key, 6)
    for position, parts in shards:
        steps = jnp.exp(jax.random.uniform(jax.random.fold_in(own, position), (parts,), jnp.float32, low / len(shards), high / len(shards)))
        loudness = loudness * jnp.repeat(steps, extent[position] // parts).reshape([-1 if axis == position else 1 for axis in range(len(extent))])
    return loudness


def normal_values(stream_key, shape, deviation, most, cuts=(), held_as=jnp.bfloat16):
    drawn = deviation * jax.random.normal(stream_key, shape, jnp.float32)
    if cuts:
        drawn = drawn * level_of(stream_key, shape, cuts, -0.22, 0.18)
    return jnp.clip(drawn, -most, most).astype(held_as)


def setup_inputs(seed: int = 0) -> dict:
    keys = jax.random.split(jax.random.key(seed), 6)
    return {
        "grid_state": normal_values(keys[0], (NLAT, NLON, C), 1.0, 6.0, ((0, 8), (1, 4))),
        "upstream": normal_values(keys[1], (NLAT, NLON, C), 1.0, 6.0, ((0, 8), (1, 4))),
        "spectral_weight": normal_values(keys[2], (C, L, 2, C), (2 * C) ** -0.5, 0.375, ((0, 4), (1, 8))),
        "up_weight": normal_values(keys[3], (C, FF), C ** -0.5, 0.5),
        "down_weight": normal_values(keys[4], (FF, C), FF ** -0.5, 0.25),
    }


def fourier_tables(lon_cells, order_ids):
    cell_ids = np.arange(lon_cells)
    phase_ids = cell_ids[:, None] * order_ids[None, :] % lon_cells
    angles = 2.0 * np.pi * phase_ids / lon_cells
    unit_scale = 2.0 * np.pi / lon_cells
    forward = np.stack([np.cos(angles) * unit_scale, -np.sin(angles) * unit_scale], axis=1)
    factor = np.where(order_ids == 0, 1.0, 2.0)[:, None]
    inverse = np.stack([np.cos(angles).T * factor, -np.sin(angles).T * factor], axis=0)
    return (forward, inverse)

def latitude_tables(lat_cells):
    cycle_ids = np.arange(lat_cells)
    colatitude = np.pi * (cycle_ids + 0.5) / lat_cells
    harmonics = np.arange(1, lat_cells // 2 + 1)
    series = np.cos(2.0 * harmonics[None, :] * colatitude[:, None]) / (4.0 * harmonics[None, :] * harmonics[None, :] - 1.0)
    quad = 2.0 / lat_cells * (1.0 - 2.0 * np.sum(series, axis=1))
    return (np.cos(colatitude), np.log(np.sin(colatitude)), quad)

def diagonal_logs(order_count):
    order_ids = np.arange(1, order_count)
    log_steps = 0.5 * np.log((2.0 * order_ids + 1.0) / (2.0 * order_ids))
    return np.concatenate([np.zeros(1), np.cumsum(log_steps)]) - 0.5 * np.log(4.0 * np.pi)

def legendre_step(carry_state, degree, orders_col, cos_row, start_logs):
    newest, former, logscale = carry_state
    degree_f = degree.astype(jnp.float32)
    is_below = degree_f < orders_col
    is_diag = degree_f == orders_col
    is_above = degree_f > orders_col
    square = orders_col * orders_col
    grow_coef = jnp.sqrt((4.0 * degree_f * degree_f - 1.0) / jnp.maximum(degree_f * degree_f - square, 1.0))
    lagged = degree_f - 1.0
    shrink = jnp.sqrt(jnp.maximum(lagged * lagged - square, 0.0) / jnp.maximum(4.0 * lagged * lagged - 1.0, 1.0))
    new_value = jnp.where(is_above, grow_coef * (cos_row * newest - shrink * former), jnp.where(is_diag, 1.0, 0.0))
    logscale = jnp.where(is_diag, start_logs, logscale)
    former = newest
    newest = new_value
    rescale = jnp.where(is_below, 1.0, jnp.maximum(jnp.abs(newest), jnp.abs(former)))
    newest = newest / rescale
    former = former / rescale
    logscale = logscale + jnp.log(rescale)
    return ((newest, former, logscale), newest * jnp.exp(logscale))

def settle(value):
    return lax.optimization_barrier(value.astype(jnp.bfloat16)).astype(jnp.float32)

def table_bf16(array):
    return lax.optimization_barrier(jnp.asarray(array, jnp.float32).astype(jnp.bfloat16)).astype(jnp.float32)

def reference(grid_state, upstream, spectral_weight, up_weight, down_weight):
    forward_np, inverse_np = fourier_tables(NLON, np.arange(M))
    fourier_fwd = table_bf16(forward_np)
    fourier_inv = table_bf16(inverse_np)
    cosines, log_sines, quad = latitude_tables(NLAT)
    cos_row = jnp.asarray(cosines, jnp.float32)[None, :]
    sin_row = jnp.asarray(log_sines, jnp.float32)[None, :]
    quad_row = jnp.asarray(quad, jnp.float32)[None, :]
    orders_col = jnp.arange(M, dtype=jnp.int32).astype(jnp.float32)[:, None]
    start_logs = jnp.asarray(diagonal_logs(M), jnp.float32)[:, None] + orders_col * sin_row
    zeros_state = jnp.zeros((M, NLAT), jnp.float32)

    def advance(carry_state, degree):
        carry_state, new_value = legendre_step(carry_state, degree, orders_col, cos_row, start_logs)
        return (carry_state, (new_value.astype(jnp.bfloat16), (new_value * quad_row).astype(jnp.bfloat16)))
    final_state, (plain, weighted) = lax.scan(advance, (zeros_state, zeros_state, zeros_state), jnp.arange(L, dtype=jnp.int32))
    plain = plain.astype(jnp.float32)
    weighted = weighted.astype(jnp.float32)
    state_f = grid_state.astype(jnp.float32)
    spectra = settle(jnp.einsum('jnc,nrm->jrmc', state_f, fourier_fwd))
    coeffs = settle(jnp.einsum('lmj,jrmc->lrmc', weighted, spectra))
    weight_f = spectral_weight.astype(jnp.float32)
    products = jnp.einsum('lrmc,dlsc->lrsmd', coeffs, weight_f)
    mixed_coeffs = settle(jnp.stack([products[:, 0, 0] - products[:, 1, 1], products[:, 0, 1] + products[:, 1, 0]], axis=1))
    cycle_values = settle(jnp.einsum('lmj,lrmc->jrmc', plain, mixed_coeffs))
    spectral_part = settle(jnp.einsum('jrmc,rmn->jnc', cycle_values, fourier_inv))
    mid_state = (state_f + spectral_part).astype(jnp.bfloat16)
    mid_rows = mid_state.reshape(-1, C)
    hidden = jnp.dot(mid_rows, up_weight, preferred_element_type=jnp.float32)
    act_value, act_pull = jax.vjp(jax.nn.gelu, hidden)
    activation = act_value.astype(jnp.bfloat16)
    next_state = (mid_rows.astype(jnp.float32) + jnp.dot(activation, down_weight, preferred_element_type=jnp.float32)).astype(jnp.bfloat16)
    next_state = next_state.reshape(NLAT, NLON, C)
    up_rows = upstream.reshape(-1, C)
    grad_down = jnp.dot(activation.T, up_rows, preferred_element_type=jnp.float32)
    pulled = jnp.dot(up_rows, down_weight.T, preferred_element_type=jnp.float32)
    grad_hidden = act_pull(pulled)[0].astype(jnp.bfloat16)
    grad_up = jnp.dot(mid_rows.T, grad_hidden, preferred_element_type=jnp.float32)
    grad_mid = (up_rows.astype(jnp.float32) + jnp.dot(grad_hidden, up_weight.T, preferred_element_type=jnp.float32)).astype(jnp.bfloat16)
    grad_mid_f = grad_mid.astype(jnp.float32).reshape(NLAT, NLON, C)
    grad_cycles = settle(jnp.einsum('jnc,rmn->jrmc', grad_mid_f, fourier_inv))
    grad_mixed = settle(jnp.einsum('lmj,jrmc->lrmc', plain, grad_cycles))
    outer = jnp.einsum('lsmd,lrmc->dlsrc', grad_mixed, coeffs)
    grad_spectral = jnp.stack([outer[:, :, 0, 0] + outer[:, :, 1, 1], outer[:, :, 1, 0] - outer[:, :, 0, 1]], axis=2)
    pulled_back = jnp.einsum('lsmd,dlrc->lsrmc', grad_mixed, weight_f)
    grad_coeffs = settle(jnp.stack([pulled_back[:, 0, 0] + pulled_back[:, 1, 1], pulled_back[:, 1, 0] - pulled_back[:, 0, 1]], axis=1))
    grad_spectra = settle(jnp.einsum('lmj,lrmc->jrmc', weighted, grad_coeffs))
    grad_spectral_part = settle(jnp.einsum('jrmc,nrm->jnc', grad_spectra, fourier_fwd))
    grad_state = (grad_mid_f + grad_spectral_part).astype(jnp.bfloat16)
    return (next_state, grad_state, grad_spectral, grad_up, grad_down)
```

```python
import jax
import jax.numpy as jnp
import numpy as np
from jax import lax
from jax.experimental import pallas as pl
from jax.experimental.pallas import tpu as pltpu
from jax.sharding import PartitionSpec as P


def fourier_tables(lon_cells, order_ids):
    cell_ids = np.arange(lon_cells)
    phase_ids = cell_ids[:, None] * order_ids[None, :] % lon_cells
    angles = 2.0 * np.pi * phase_ids / lon_cells
    unit_scale = 2.0 * np.pi / lon_cells
    forward = np.stack([np.cos(angles) * unit_scale, -np.sin(angles) * unit_scale], axis=1)
    factor = np.where(order_ids == 0, 1.0, 2.0)[:, None]
    inverse = np.stack([np.cos(angles).T * factor, -np.sin(angles).T * factor], axis=0)
    return (forward, inverse)


def latitude_tables(lat_cells):
    cycle_ids = np.arange(lat_cells)
    colatitude = np.pi * (cycle_ids + 0.5) / lat_cells
    harmonics = np.arange(1, lat_cells // 2 + 1)
    series = np.cos(2.0 * harmonics[None, :] * colatitude[:, None]) / (
        4.0 * harmonics[None, :] * harmonics[None, :] - 1.0
    )
    quad = 2.0 / lat_cells * (1.0 - 2.0 * np.sum(series, axis=1))
    return (np.cos(colatitude), np.log(np.sin(colatitude)), quad)


def diagonal_logs(order_count):
    order_ids = np.arange(1, order_count)
    log_steps = 0.5 * np.log((2.0 * order_ids + 1.0) / (2.0 * order_ids))
    return np.concatenate([np.zeros(1), np.cumsum(log_steps)]) - 0.5 * np.log(4.0 * np.pi)


def legendre_step(carry_state, degree, orders_col, cos_row, start_logs):
    newest, former, logscale = carry_state
    degree_f = degree.astype(jnp.float32)
    is_below = degree_f < orders_col
    is_diag = degree_f == orders_col
    is_above = degree_f > orders_col
    square = orders_col * orders_col
    grow_coef = jnp.sqrt(
        (4.0 * degree_f * degree_f - 1.0) / jnp.maximum(degree_f * degree_f - square, 1.0)
    )
    lagged = degree_f - 1.0
    shrink = jnp.sqrt(
        jnp.maximum(lagged * lagged - square, 0.0) / jnp.maximum(4.0 * lagged * lagged - 1.0, 1.0)
    )
    new_value = jnp.where(
        is_above, grow_coef * (cos_row * newest - shrink * former), jnp.where(is_diag, 1.0, 0.0)
    )
    logscale = jnp.where(is_diag, start_logs, logscale)
    former = newest
    newest = new_value
    rescale = jnp.where(is_below, 1.0, jnp.maximum(jnp.abs(newest), jnp.abs(former)))
    newest = newest / rescale
    former = former / rescale
    logscale = logscale + jnp.log(rescale)
    return ((newest, former, logscale), newest * jnp.exp(logscale))


def legendre_tables(orders_col, start_logs, cos_row, quad_row, degrees):
    unroll = 16
    zeros_state = jnp.zeros((orders_col.shape[0], cos_row.shape[1]), jnp.float32)

    def advance(carry_state, opening):
        collected = []
        for offset in range(unroll):
            carry_state, new_value = legendre_step(
                carry_state, opening + offset, orders_col, cos_row, start_logs
            )
            collected.append(new_value)
        stacked = jnp.stack(collected)
        return (
            carry_state,
            (stacked.astype(jnp.bfloat16), (stacked * quad_row).astype(jnp.bfloat16)),
        )

    openings = jnp.arange(0, degrees, unroll, dtype=jnp.int32)
    final_state, (plain, weighted) = lax.scan(
        advance, (zeros_state, zeros_state, zeros_state), openings
    )
    full_shape = (degrees, orders_col.shape[0], cos_row.shape[1])
    return (plain.reshape(full_shape), weighted.reshape(full_shape))


def order_slots(degrees):
    slot_ids = np.arange(degrees)
    return slot_ids


def degree_blocks(degrees, per_device):
    return [(0, degrees, per_device)]


def to_degrees(cycle_input, basis_table, blocks):
    order_total = cycle_input.shape[2]
    pieces_list = []
    for opening, block_size, needed in blocks:
        block_part = jnp.einsum(
            "lkj,jrkc->lrkc",
            basis_table[opening : opening + block_size, :needed],
            cycle_input[:, :, :needed],
            preferred_element_type=jnp.float32,
        )
        if needed < order_total:
            block_part = jnp.pad(block_part, ((0, 0), (0, 0), (0, order_total - needed), (0, 0)))
        pieces_list.append(block_part)
    return jnp.concatenate(pieces_list, axis=0).astype(jnp.bfloat16)


def to_latitudes(degree_input, basis_table, blocks):
    order_total = degree_input.shape[2]
    accum = None
    for opening, block_size, needed in blocks:
        block_part = jnp.einsum(
            "lkj,lrkc->jrkc",
            basis_table[opening : opening + block_size, :needed],
            degree_input[opening : opening + block_size, :, :needed],
            preferred_element_type=jnp.float32,
        )
        if needed < order_total:
            block_part = jnp.pad(block_part, ((0, 0), (0, 0), (0, order_total - needed), (0, 0)))
        accum = block_part
    return accum.astype(jnp.bfloat16)


def grid_to_orders(grid_values, fourier_table, letters):
    spectrum = jnp.einsum(
        letters,
        lax.all_to_all(grid_values, "lon", split_axis=2, concat_axis=1, tiled=True),
        fourier_table,
        preferred_element_type=jnp.float32,
    ).astype(jnp.bfloat16)
    return lax.all_to_all(spectrum, "lon", split_axis=2, concat_axis=3, tiled=True)


def orders_to_grid(order_values, fourier_table, letters):
    columns = jnp.einsum(
        letters,
        lax.all_to_all(order_values, "lon", split_axis=3, concat_axis=2, tiled=True),
        fourier_table,
        preferred_element_type=jnp.float32,
    ).astype(jnp.bfloat16)
    return lax.all_to_all(columns, "lon", split_axis=1, concat_axis=2, tiled=True)


def to_spectral(order_values, basis_table, blocks):
    cycle_input = lax.all_to_all(order_values, "lat", split_axis=3, concat_axis=0, tiled=True)
    degree_values = to_degrees(cycle_input, basis_table, blocks)
    return lax.all_to_all(degree_values, "lat", split_axis=0, concat_axis=3, tiled=True)


def from_spectral(degree_values, basis_table, blocks):
    degree_input = lax.all_to_all(degree_values, "lat", split_axis=3, concat_axis=0, tiled=True)
    cycle_values = to_latitudes(degree_input, basis_table, blocks)
    return lax.all_to_all(cycle_values, "lat", split_axis=0, concat_axis=3, tiled=True)


def forward_mix(coeffs, weight_piece):
    products = jnp.einsum(
        "lrkc,dlsc->lrskd", coeffs, weight_piece, preferred_element_type=jnp.float32
    )
    real_part = products[:, 0, 0] - products[:, 1, 1]
    imag_part = products[:, 0, 1] + products[:, 1, 0]
    return jnp.stack([real_part, imag_part], axis=1)


def back_mix(grad_part, weight_piece):
    products = jnp.einsum(
        "lskd,dlrc->lsrkc", grad_part, weight_piece, preferred_element_type=jnp.float32
    )
    real_part = products[:, 0, 0] + products[:, 1, 1]
    imag_part = products[:, 1, 0] - products[:, 0, 1]
    return jnp.stack([real_part, imag_part], axis=1)


def weight_grad(coeffs, grad_part):
    products = jnp.einsum("lskd,lrkc->dlsrc", grad_part, coeffs, preferred_element_type=jnp.float32)
    real_part = products[:, :, 0, 0] + products[:, :, 1, 1]
    imag_part = products[:, :, 1, 0] - products[:, :, 0, 1]
    return jnp.stack([real_part, imag_part], axis=2)


def general_device(grid_state, upstream, spectral_weight, up_weight, down_weight):
    lat_devices = lax.axis_size("lat")
    lon_devices = lax.axis_size("lon")
    lat_rows, lon_cells, channels = grid_state.shape
    degrees = lat_rows * lat_devices
    lon_total = lon_cells * lon_devices
    per_device = degrees // lon_devices
    forward_np, inverse_np = fourier_tables(lon_total, order_slots(degrees))
    fourier_fwd = jnp.asarray(forward_np, jnp.float32).astype(jnp.bfloat16)
    fourier_inv = jnp.asarray(inverse_np, jnp.float32).astype(jnp.bfloat16)
    cosines, log_sines, quad = latitude_tables(degrees)
    cos_row = jnp.asarray(cosines, jnp.float32)[None, :]
    sin_row = jnp.asarray(log_sines, jnp.float32)[None, :]
    quad_row = jnp.asarray(quad, jnp.float32)[None, :]
    lon_index = lax.axis_index("lon")
    counter = jnp.arange(per_device, dtype=jnp.int32)
    order_ids = lon_index * per_device + counter
    diag_row = jnp.asarray(diagonal_logs(degrees), jnp.float32)[None, :]
    matches = order_ids[:, None] == jnp.arange(degrees, dtype=jnp.int32)[None, :]
    picked = jnp.sum(jnp.where(matches, diag_row, 0.0), axis=1)
    orders_col = order_ids.astype(jnp.float32)[:, None]
    start_logs = picked[:, None] + orders_col * sin_row
    plain, weighted = legendre_tables(orders_col, start_logs, cos_row, quad_row, degrees)
    blocks = degree_blocks(degrees, per_device)
    spectra = grid_to_orders(grid_state, fourier_fwd, "knc,nrs->krsc")
    coeffs = to_spectral(spectra, weighted, blocks)
    mixed_coeffs = forward_mix(
        coeffs, lax.all_gather(spectral_weight, "lon", axis=0, tiled=True)
    ).astype(jnp.bfloat16)
    cycle_values = from_spectral(mixed_coeffs, plain, blocks)
    spectral_part = orders_to_grid(cycle_values, fourier_inv, "krsc,rsn->knc")
    mid_state = (grid_state.astype(jnp.float32) + spectral_part.astype(jnp.float32)).astype(
        jnp.bfloat16
    )
    mid_rows = mid_state.reshape(-1, channels)
    hidden = jnp.dot(mid_rows, up_weight, preferred_element_type=jnp.float32)
    act_value, act_pull = jax.vjp(jax.nn.gelu, hidden)
    activation = act_value.astype(jnp.bfloat16)
    next_rows = mid_rows.astype(jnp.float32) + jnp.dot(
        activation, down_weight, preferred_element_type=jnp.float32
    )
    next_state = next_rows.astype(jnp.bfloat16).reshape(lat_rows, lon_cells, channels)
    up_rows = upstream.reshape(-1, channels)
    down_part = jnp.einsum("tf,tc->fc", activation, up_rows, preferred_element_type=jnp.float32)
    pulled = jnp.einsum("tc,fc->tf", up_rows, down_weight, preferred_element_type=jnp.float32)
    grad_hidden = act_pull(pulled)[0].astype(jnp.bfloat16)
    up_part = jnp.einsum("tc,tf->cf", mid_rows, grad_hidden, preferred_element_type=jnp.float32)
    grad_mid = up_rows.astype(jnp.float32) + jnp.einsum(
        "tf,cf->tc", grad_hidden, up_weight, preferred_element_type=jnp.float32
    )
    grad_mid = grad_mid.astype(jnp.bfloat16).reshape(lat_rows, lon_cells, channels)
    grad_up, grad_down = lax.psum((up_part, down_part), ("lat", "lon"))
    grad_cycles = grid_to_orders(grad_mid, fourier_inv, "knc,rsn->krsc")
    grad_mixed = to_spectral(grad_cycles, plain, blocks)
    grad_part = lax.slice_in_dim(
        grad_mixed, 0, channels // lon_devices * lax.axis_size("lon"), axis=3
    )
    grad_spectral = lax.psum_scatter(
        weight_grad(coeffs, grad_part).astype(jnp.bfloat16), "lon", scatter_dimension=0, tiled=True
    ).astype(jnp.float32)
    initial = jnp.zeros(coeffs.shape, jnp.float32)
    weight_piece = lax.all_gather(spectral_weight, "lon", axis=0, tiled=True)
    grad_part = lax.slice_in_dim(grad_mixed, 0, weight_piece.shape[0], axis=3)
    grad_coeffs = (initial + back_mix(grad_part, weight_piece)).astype(jnp.bfloat16)
    grad_spectra = from_spectral(grad_coeffs, weighted, blocks)
    grad_spectral_part = orders_to_grid(grad_spectra, fourier_fwd, "krsc,nrs->knc")
    grad_state = (grad_mid.astype(jnp.float32) + grad_spectral_part.astype(jnp.float32)).astype(
        jnp.bfloat16
    )
    return (next_state, grad_state, grad_spectral, grad_up, grad_down)


GROUP = 8


def table_kernel(orders, degrees, cos_ref, start_ref, grow_ref, lag_ref, seed_ref, out_ref, held):
    cos_rows = cos_ref[...]
    zeros = jnp.zeros(start_ref.shape, jnp.float32)

    def advance(block, carry):
        newest, former, logscale = carry
        scale = jnp.exp(logscale)
        for offset in range(GROUP):
            degree = block * GROUP + offset
            value = (
                cos_rows * grow_ref[degree] * newest - lag_ref[degree] * former + seed_ref[degree]
            )
            former = newest
            newest = value
            held[degree] = value * scale
        top = jnp.maximum(jnp.abs(newest), jnp.abs(former))
        top = jnp.where(top == 0.0, 1.0, top)
        return (newest / top, former / top, logscale + jnp.log(top))

    lax.fori_loop(0, degrees // GROUP, advance, (zeros, zeros, start_ref[...]))
    for order in range(orders):
        out_ref[order] = held[:, order, :].astype(jnp.bfloat16)


def order_table(order_ids, degrees, cosines, log_sines):
    orders = order_ids.shape[0]
    padded = -(-orders // 8) * 8
    ids = jnp.concatenate([order_ids, jnp.full((padded - orders,), degrees, jnp.int32)])
    diag_row = jnp.asarray(diagonal_logs(degrees), jnp.float32)[None, :]
    matches = ids[:, None] == jnp.arange(degrees, dtype=jnp.int32)[None, :]
    picked = jnp.sum(jnp.where(matches, diag_row, 0.0), axis=1)
    orders_row = ids.astype(jnp.float32)
    cos_row = jnp.asarray(cosines, jnp.float32)[None, :]
    sin_row = jnp.asarray(log_sines, jnp.float32)[None, :]
    start_logs = picked[:, None] + orders_row[:, None] * sin_row
    degree_col = jnp.arange(degrees, dtype=jnp.float32)[:, None]
    square = orders_row[None, :] * orders_row[None, :]
    grow = jnp.sqrt(
        (4.0 * degree_col * degree_col - 1.0) / jnp.maximum(degree_col * degree_col - square, 1.0)
    )
    grow = jnp.where(degree_col > orders_row[None, :], grow, 0.0)
    lagged = degree_col - 1.0
    shrink = jnp.sqrt(
        jnp.maximum(lagged * lagged - square, 0.0) / jnp.maximum(4.0 * lagged * lagged - 1.0, 1.0)
    )
    seed = jnp.where(degree_col == orders_row[None, :], 1.0, 0.0)
    cycles = cos_row.shape[1]
    return pl.pallas_call(
        lambda *refs: table_kernel(orders, degrees, *refs),
        out_shape=jax.ShapeDtypeStruct((orders, degrees, cycles), jnp.bfloat16),
        in_specs=[pl.BlockSpec(memory_space=pltpu.VMEM)] * 5,
        out_specs=pl.BlockSpec(memory_space=pltpu.VMEM),
        scratch_shapes=[pltpu.VMEM((degrees, padded, cycles), jnp.float32)],
        compiler_params=pltpu.CompilerParams(vmem_limit_bytes=48 * 2**20),
        cost_estimate=pl.CostEstimate(
            flops=12 * degrees * padded * cycles,
            bytes_accessed=2 * orders * degrees * cycles,
            transcendentals=0,
        ),
    )(
        jnp.broadcast_to(cos_row, start_logs.shape),
        start_logs,
        grow[:, :, None],
        (grow * shrink)[:, :, None],
        seed[:, :, None],
    )


def on_device(grid_state, upstream, spectral_weight, up_weight, down_weight):
    lat_devices = lax.axis_size("lat")
    lon_devices = lax.axis_size("lon")
    lat_rows, lon_cells, channels = grid_state.shape
    degrees = lat_rows * lat_devices
    if lat_rows % lon_devices or (degrees // (lat_devices * lon_devices)) % 4:
        return general_device(grid_state, upstream, spectral_weight, up_weight, down_weight)
    devices = lat_devices * lon_devices
    orders = degrees // devices
    cycles = lat_rows // lon_devices
    lon_total = lon_cells * lon_devices
    both = ("lat", "lon")
    place = lax.axis_index("lat") * lon_devices + lax.axis_index("lon")

    forward_np, inverse_np = fourier_tables(lon_total, order_slots(degrees))

    def by_order(table):
        table = table.reshape(lon_total, 2, devices, orders).transpose(0, 2, 1, 3)
        return jnp.asarray(table.reshape(lon_total, 2 * degrees), jnp.float32).astype(jnp.bfloat16)

    fourier_fwd = by_order(forward_np)
    fourier_inv = by_order(inverse_np.transpose(2, 0, 1))
    cosines, log_sines, quad = latitude_tables(degrees)
    quad_all = jnp.asarray(quad, jnp.float32)
    quad_own = lax.dynamic_slice_in_dim(quad_all, place * cycles, cycles, axis=0)
    order_ids = place * orders + jnp.arange(orders, dtype=jnp.int32)
    table = order_table(order_ids, degrees, cosines, log_sines)
    weight = lax.all_gather(spectral_weight, "lon", axis=0, tiled=True)

    def grid_to_degrees(values, fourier, scale):
        circles = lax.all_to_all(values, "lon", split_axis=0, concat_axis=1, tiled=True)
        spectrum = jnp.einsum("jnc,nq->jqc", circles, fourier, preferred_element_type=jnp.float32)
        if scale is not None:
            spectrum = spectrum * scale[:, None, None]
        spectrum = lax.all_to_all(
            spectrum.astype(jnp.bfloat16), both, split_axis=1, concat_axis=0, tiled=True
        ).reshape(degrees, 2, orders, channels)
        coeffs = jnp.einsum(
            "mlj,jrmc->lrmc", table, spectrum, preferred_element_type=jnp.float32
        ).astype(jnp.bfloat16)
        coeffs = lax.all_to_all(
            coeffs.reshape(lat_devices, lat_rows, 2 * orders, channels), "lat", 0, 0, tiled=True
        ).reshape(lat_devices, lat_rows, 2, orders, channels)
        return coeffs.transpose(1, 2, 0, 3, 4).reshape(
            lat_rows, 2, lat_devices * orders, channels
        )

    def degrees_to_grid(coeffs, fourier, scale):
        coeffs = coeffs.reshape(lat_rows, 2, lat_devices, orders, channels).transpose(2, 0, 1, 3, 4)
        coeffs = lax.all_to_all(
            coeffs.reshape(lat_devices, lat_rows, 2 * orders, channels), "lat", 0, 0, tiled=True
        ).reshape(degrees, 2, orders, channels)
        spectrum = jnp.einsum("mlj,lrmc->jrmc", table, coeffs, preferred_element_type=jnp.float32)
        if scale is not None:
            spectrum = spectrum * scale[:, None, None, None]
        spectrum = lax.all_to_all(
            spectrum.astype(jnp.bfloat16).reshape(degrees, 2 * orders, channels),
            both,
            split_axis=0,
            concat_axis=1,
            tiled=True,
        )
        circles = jnp.einsum("jqc,nq->jnc", spectrum, fourier, preferred_element_type=jnp.float32)
        return lax.all_to_all(
            circles.astype(jnp.bfloat16), "lon", split_axis=1, concat_axis=0, tiled=True
        )

    coeffs = grid_to_degrees(grid_state, fourier_fwd, quad_own)
    mixed_coeffs = forward_mix(coeffs, weight).astype(jnp.bfloat16)
    spectral_part = degrees_to_grid(mixed_coeffs, fourier_inv, None)
    mid_state = (grid_state.astype(jnp.float32) + spectral_part.astype(jnp.float32)).astype(
        jnp.bfloat16
    )
    mid_rows = mid_state.reshape(-1, channels)
    hidden = jnp.dot(mid_rows, up_weight, preferred_element_type=jnp.float32)
    act_value, act_pull = jax.vjp(jax.nn.gelu, hidden)
    activation = act_value.astype(jnp.bfloat16)
    next_rows = mid_rows.astype(jnp.float32) + jnp.dot(
        activation, down_weight, preferred_element_type=jnp.float32
    )
    next_state = next_rows.astype(jnp.bfloat16).reshape(lat_rows, lon_cells, channels)
    up_rows = upstream.reshape(-1, channels)
    down_part = jnp.einsum("tf,tc->fc", activation, up_rows, preferred_element_type=jnp.float32)
    pulled = jnp.einsum("tc,fc->tf", up_rows, down_weight, preferred_element_type=jnp.float32)
    grad_hidden = act_pull(pulled)[0].astype(jnp.bfloat16)
    up_part = jnp.einsum("tc,tf->cf", mid_rows, grad_hidden, preferred_element_type=jnp.float32)
    grad_mid = up_rows.astype(jnp.float32) + jnp.einsum(
        "tf,cf->tc", grad_hidden, up_weight, preferred_element_type=jnp.float32
    )
    grad_mid = grad_mid.astype(jnp.bfloat16).reshape(lat_rows, lon_cells, channels)
    grad_mid, up_part, down_part, next_state = lax.optimization_barrier(
        (grad_mid, up_part, down_part, next_state)
    )
    grad_up, grad_down = lax.psum((up_part, down_part), both)
    grad_mixed = grid_to_degrees(grad_mid, fourier_inv, None)
    grad_spectral = lax.psum_scatter(
        weight_grad(coeffs, grad_mixed).astype(jnp.bfloat16), "lon", scatter_dimension=0, tiled=True
    ).astype(jnp.float32)
    grad_coeffs = back_mix(grad_mixed, weight).astype(jnp.bfloat16)
    grad_spectral_part = degrees_to_grid(grad_coeffs, fourier_fwd, quad_all)
    grad_state = (grad_mid.astype(jnp.float32) + grad_spectral_part.astype(jnp.float32)).astype(
        jnp.bfloat16
    )
    return (next_state, grad_state, grad_spectral, grad_up, grad_down)


def solution(mesh):
    in_specs = (P("lat", "lon", None), P("lat", "lon", None), P("lon", "lat", None, None), P(), P())
    out_specs = (
        P("lat", "lon", None),
        P("lat", "lon", None),
        P("lon", "lat", None, None),
        P(),
        P(),
    )
    return jax.shard_map(
        on_device, mesh=mesh, in_specs=in_specs, out_specs=out_specs, check_vma=False
    )
```

```python
import jax
import jax.numpy as jnp
import numpy as np
from jax import lax
from jax.experimental import pallas as pl
from jax.experimental.pallas import tpu as pltpu
from jax.sharding import PartitionSpec as P


def fourier_tables(lon_cells, order_ids):
    cell_ids = np.arange(lon_cells)
    phase_ids = cell_ids[:, None] * order_ids[None, :] % lon_cells
    angles = 2.0 * np.pi * phase_ids / lon_cells
    unit_scale = 2.0 * np.pi / lon_cells
    forward = np.stack([np.cos(angles) * unit_scale, -np.sin(angles) * unit_scale], axis=1)
    factor = np.where(order_ids == 0, 1.0, 2.0)[:, None]
    inverse = np.stack([np.cos(angles).T * factor, -np.sin(angles).T * factor], axis=0)
    return (forward, inverse)


def latitude_tables(lat_cells):
    cycle_ids = np.arange(lat_cells)
    colatitude = np.pi * (cycle_ids + 0.5) / lat_cells
    harmonics = np.arange(1, lat_cells // 2 + 1)
    series = np.cos(2.0 * harmonics[None, :] * colatitude[:, None]) / (
        4.0 * harmonics[None, :] * harmonics[None, :] - 1.0
    )
    quad = 2.0 / lat_cells * (1.0 - 2.0 * np.sum(series, axis=1))
    return (np.cos(colatitude), np.log(np.sin(colatitude)), quad)


def diagonal_logs(order_count):
    order_ids = np.arange(1, order_count)
    log_steps = 0.5 * np.log((2.0 * order_ids + 1.0) / (2.0 * order_ids))
    return np.concatenate([np.zeros(1), np.cumsum(log_steps)]) - 0.5 * np.log(4.0 * np.pi)


def legendre_step(carry_state, degree, orders_col, cos_row, start_logs):
    newest, former, logscale = carry_state
    degree_f = degree.astype(jnp.float32)
    is_below = degree_f < orders_col
    is_diag = degree_f == orders_col
    is_above = degree_f > orders_col
    square = orders_col * orders_col
    grow_coef = jnp.sqrt(
        (4.0 * degree_f * degree_f - 1.0) / jnp.maximum(degree_f * degree_f - square, 1.0)
    )
    lagged = degree_f - 1.0
    shrink = jnp.sqrt(
        jnp.maximum(lagged * lagged - square, 0.0) / jnp.maximum(4.0 * lagged * lagged - 1.0, 1.0)
    )
    new_value = jnp.where(
        is_above, grow_coef * (cos_row * newest - shrink * former), jnp.where(is_diag, 1.0, 0.0)
    )
    logscale = jnp.where(is_diag, start_logs, logscale)
    former = newest
    newest = new_value
    rescale = jnp.where(is_below, 1.0, jnp.maximum(jnp.abs(newest), jnp.abs(former)))
    newest = newest / rescale
    former = former / rescale
    logscale = logscale + jnp.log(rescale)
    return ((newest, former, logscale), newest * jnp.exp(logscale))


def legendre_tables(orders_col, start_logs, cos_row, quad_row, degrees):
    unroll = 16
    zeros_state = jnp.zeros((orders_col.shape[0], cos_row.shape[1]), jnp.float32)

    def advance(carry_state, opening):
        collected = []
        for offset in range(unroll):
            carry_state, new_value = legendre_step(
                carry_state, opening + offset, orders_col, cos_row, start_logs
            )
            collected.append(new_value)
        stacked = jnp.stack(collected)
        return (
            carry_state,
            (stacked.astype(jnp.bfloat16), (stacked * quad_row).astype(jnp.bfloat16)),
        )

    openings = jnp.arange(0, degrees, unroll, dtype=jnp.int32)
    final_state, (plain, weighted) = lax.scan(
        advance, (zeros_state, zeros_state, zeros_state), openings
    )
    full_shape = (degrees, orders_col.shape[0], cos_row.shape[1])
    return (plain.reshape(full_shape), weighted.reshape(full_shape))


def order_slots(degrees):
    slot_ids = np.arange(degrees)
    return slot_ids


def degree_blocks(degrees, per_device):
    return [(0, degrees, per_device)]


def to_degrees(cycle_input, basis_table, blocks):
    order_total = cycle_input.shape[2]
    pieces_list = []
    for opening, block_size, needed in blocks:
        block_part = jnp.einsum(
            "lkj,jrkc->lrkc",
            basis_table[opening : opening + block_size, :needed],
            cycle_input[:, :, :needed],
            preferred_element_type=jnp.float32,
        )
        if needed < order_total:
            block_part = jnp.pad(block_part, ((0, 0), (0, 0), (0, order_total - needed), (0, 0)))
        pieces_list.append(block_part)
    return jnp.concatenate(pieces_list, axis=0).astype(jnp.bfloat16)


def to_latitudes(degree_input, basis_table, blocks):
    order_total = degree_input.shape[2]
    accum = None
    for opening, block_size, needed in blocks:
        block_part = jnp.einsum(
            "lkj,lrkc->jrkc",
            basis_table[opening : opening + block_size, :needed],
            degree_input[opening : opening + block_size, :, :needed],
            preferred_element_type=jnp.float32,
        )
        if needed < order_total:
            block_part = jnp.pad(block_part, ((0, 0), (0, 0), (0, order_total - needed), (0, 0)))
        accum = block_part
    return accum.astype(jnp.bfloat16)


def grid_to_orders(grid_values, fourier_table, letters):
    spectrum = jnp.einsum(
        letters,
        lax.all_to_all(grid_values, "lon", split_axis=2, concat_axis=1, tiled=True),
        fourier_table,
        preferred_element_type=jnp.float32,
    ).astype(jnp.bfloat16)
    return lax.all_to_all(spectrum, "lon", split_axis=2, concat_axis=3, tiled=True)


def orders_to_grid(order_values, fourier_table, letters):
    columns = jnp.einsum(
        letters,
        lax.all_to_all(order_values, "lon", split_axis=3, concat_axis=2, tiled=True),
        fourier_table,
        preferred_element_type=jnp.float32,
    ).astype(jnp.bfloat16)
    return lax.all_to_all(columns, "lon", split_axis=1, concat_axis=2, tiled=True)


def to_spectral(order_values, basis_table, blocks):
    cycle_input = lax.all_to_all(order_values, "lat", split_axis=3, concat_axis=0, tiled=True)
    degree_values = to_degrees(cycle_input, basis_table, blocks)
    return lax.all_to_all(degree_values, "lat", split_axis=0, concat_axis=3, tiled=True)


def from_spectral(degree_values, basis_table, blocks):
    degree_input = lax.all_to_all(degree_values, "lat", split_axis=3, concat_axis=0, tiled=True)
    cycle_values = to_latitudes(degree_input, basis_table, blocks)
    return lax.all_to_all(cycle_values, "lat", split_axis=0, concat_axis=3, tiled=True)


def forward_mix(coeffs, weight_piece):
    products = jnp.einsum(
        "lrkc,dlsc->lrskd", coeffs, weight_piece, preferred_element_type=jnp.float32
    )
    real_part = products[:, 0, 0] - products[:, 1, 1]
    imag_part = products[:, 0, 1] + products[:, 1, 0]
    return jnp.stack([real_part, imag_part], axis=1)


def back_mix(grad_part, weight_piece):
    products = jnp.einsum(
        "lskd,dlrc->lsrkc", grad_part, weight_piece, preferred_element_type=jnp.float32
    )
    real_part = products[:, 0, 0] + products[:, 1, 1]
    imag_part = products[:, 1, 0] - products[:, 0, 1]
    return jnp.stack([real_part, imag_part], axis=1)


def weight_grad(coeffs, grad_part):
    products = jnp.einsum("lskd,lrkc->dlsrc", grad_part, coeffs, preferred_element_type=jnp.float32)
    real_part = products[:, :, 0, 0] + products[:, :, 1, 1]
    imag_part = products[:, :, 1, 0] - products[:, :, 0, 1]
    return jnp.stack([real_part, imag_part], axis=2)


def general_device(grid_state, upstream, spectral_weight, up_weight, down_weight):
    lat_devices = lax.axis_size("lat")
    lon_devices = lax.axis_size("lon")
    lat_rows, lon_cells, channels = grid_state.shape
    degrees = lat_rows * lat_devices
    lon_total = lon_cells * lon_devices
    per_device = degrees // lon_devices
    forward_np, inverse_np = fourier_tables(lon_total, order_slots(degrees))
    fourier_fwd = jnp.asarray(forward_np, jnp.float32).astype(jnp.bfloat16)
    fourier_inv = jnp.asarray(inverse_np, jnp.float32).astype(jnp.bfloat16)
    cosines, log_sines, quad = latitude_tables(degrees)
    cos_row = jnp.asarray(cosines, jnp.float32)[None, :]
    sin_row = jnp.asarray(log_sines, jnp.float32)[None, :]
    quad_row = jnp.asarray(quad, jnp.float32)[None, :]
    lon_index = lax.axis_index("lon")
    counter = jnp.arange(per_device, dtype=jnp.int32)
    order_ids = lon_index * per_device + counter
    diag_row = jnp.asarray(diagonal_logs(degrees), jnp.float32)[None, :]
    matches = order_ids[:, None] == jnp.arange(degrees, dtype=jnp.int32)[None, :]
    picked = jnp.sum(jnp.where(matches, diag_row, 0.0), axis=1)
    orders_col = order_ids.astype(jnp.float32)[:, None]
    start_logs = picked[:, None] + orders_col * sin_row
    plain, weighted = legendre_tables(orders_col, start_logs, cos_row, quad_row, degrees)
    blocks = degree_blocks(degrees, per_device)
    spectra = grid_to_orders(grid_state, fourier_fwd, "knc,nrs->krsc")
    coeffs = to_spectral(spectra, weighted, blocks)
    mixed_coeffs = forward_mix(
        coeffs, lax.all_gather(spectral_weight, "lon", axis=0, tiled=True)
    ).astype(jnp.bfloat16)
    cycle_values = from_spectral(mixed_coeffs, plain, blocks)
    spectral_part = orders_to_grid(cycle_values, fourier_inv, "krsc,rsn->knc")
    mid_state = (grid_state.astype(jnp.float32) + spectral_part.astype(jnp.float32)).astype(
        jnp.bfloat16
    )
    mid_rows = mid_state.reshape(-1, channels)
    hidden = jnp.dot(mid_rows, up_weight, preferred_element_type=jnp.float32)
    act_value, act_pull = jax.vjp(jax.nn.gelu, hidden)
    activation = act_value.astype(jnp.bfloat16)
    next_rows = mid_rows.astype(jnp.float32) + jnp.dot(
        activation, down_weight, preferred_element_type=jnp.float32
    )
    next_state = next_rows.astype(jnp.bfloat16).reshape(lat_rows, lon_cells, channels)
    up_rows = upstream.reshape(-1, channels)
    down_part = jnp.einsum("tf,tc->fc", activation, up_rows, preferred_element_type=jnp.float32)
    pulled = jnp.einsum("tc,fc->tf", up_rows, down_weight, preferred_element_type=jnp.float32)
    grad_hidden = act_pull(pulled)[0].astype(jnp.bfloat16)
    up_part = jnp.einsum("tc,tf->cf", mid_rows, grad_hidden, preferred_element_type=jnp.float32)
    grad_mid = up_rows.astype(jnp.float32) + jnp.einsum(
        "tf,cf->tc", grad_hidden, up_weight, preferred_element_type=jnp.float32
    )
    grad_mid = grad_mid.astype(jnp.bfloat16).reshape(lat_rows, lon_cells, channels)
    grad_up, grad_down = lax.psum((up_part, down_part), ("lat", "lon"))
    grad_cycles = grid_to_orders(grad_mid, fourier_inv, "knc,rsn->krsc")
    grad_mixed = to_spectral(grad_cycles, plain, blocks)
    grad_part = lax.slice_in_dim(
        grad_mixed, 0, channels // lon_devices * lax.axis_size("lon"), axis=3
    )
    grad_spectral = lax.psum_scatter(
        weight_grad(coeffs, grad_part).astype(jnp.bfloat16), "lon", scatter_dimension=0, tiled=True
    ).astype(jnp.float32)
    initial = jnp.zeros(coeffs.shape, jnp.float32)
    weight_piece = lax.all_gather(spectral_weight, "lon", axis=0, tiled=True)
    grad_part = lax.slice_in_dim(grad_mixed, 0, weight_piece.shape[0], axis=3)
    grad_coeffs = (initial + back_mix(grad_part, weight_piece)).astype(jnp.bfloat16)
    grad_spectra = from_spectral(grad_coeffs, weighted, blocks)
    grad_spectral_part = orders_to_grid(grad_spectra, fourier_fwd, "krsc,nrs->knc")
    grad_state = (grad_mid.astype(jnp.float32) + grad_spectral_part.astype(jnp.float32)).astype(
        jnp.bfloat16
    )
    return (next_state, grad_state, grad_spectral, grad_up, grad_down)


GROUP = 8


def table_kernel(orders, degrees, cos_ref, start_ref, grow_ref, lag_ref, seed_ref, out_ref, held):
    cos_rows = cos_ref[...]
    zeros = jnp.zeros(start_ref.shape, jnp.float32)

    def advance(block, carry):
        newest, former, logscale = carry
        scale = jnp.exp(logscale)
        for offset in range(GROUP):
            degree = block * GROUP + offset
            value = (
                cos_rows * grow_ref[degree] * newest - lag_ref[degree] * former + seed_ref[degree]
            )
            former = newest
            newest = value
            held[degree] = value * scale
        top = jnp.maximum(jnp.abs(newest), jnp.abs(former))
        top = jnp.where(top == 0.0, 1.0, top)
        return (newest / top, former / top, logscale + jnp.log(top))

    lax.fori_loop(0, degrees // GROUP, advance, (zeros, zeros, start_ref[...]))
    for order in range(orders):
        out_ref[order] = held[:, order, :].astype(jnp.bfloat16)


def order_table(order_ids, degrees, cosines, log_sines):
    orders = order_ids.shape[0]
    padded = -(-orders // 8) * 8
    ids = jnp.concatenate([order_ids, jnp.full((padded - orders,), degrees, jnp.int32)])
    diag_row = jnp.asarray(diagonal_logs(degrees), jnp.float32)[None, :]
    matches = ids[:, None] == jnp.arange(degrees, dtype=jnp.int32)[None, :]
    picked = jnp.sum(jnp.where(matches, diag_row, 0.0), axis=1)
    orders_row = ids.astype(jnp.float32)
    cos_row = jnp.asarray(cosines, jnp.float32)[None, :]
    sin_row = jnp.asarray(log_sines, jnp.float32)[None, :]
    start_logs = picked[:, None] + orders_row[:, None] * sin_row
    degree_col = jnp.arange(degrees, dtype=jnp.float32)[:, None]
    square = orders_row[None, :] * orders_row[None, :]
    grow = jnp.sqrt(
        (4.0 * degree_col * degree_col - 1.0) / jnp.maximum(degree_col * degree_col - square, 1.0)
    )
    grow = jnp.where(degree_col > orders_row[None, :], grow, 0.0)
    lagged = degree_col - 1.0
    shrink = jnp.sqrt(
        jnp.maximum(lagged * lagged - square, 0.0) / jnp.maximum(4.0 * lagged * lagged - 1.0, 1.0)
    )
    seed = jnp.where(degree_col == orders_row[None, :], 1.0, 0.0)
    cycles = cos_row.shape[1]
    return pl.pallas_call(
        lambda *refs: table_kernel(orders, degrees, *refs),
        out_shape=jax.ShapeDtypeStruct((orders, degrees, cycles), jnp.bfloat16),
        in_specs=[pl.BlockSpec(memory_space=pltpu.VMEM)] * 5,
        out_specs=pl.BlockSpec(memory_space=pltpu.VMEM),
        scratch_shapes=[pltpu.VMEM((degrees, padded, cycles), jnp.float32)],
        compiler_params=pltpu.CompilerParams(vmem_limit_bytes=48 * 2**20),
        cost_estimate=pl.CostEstimate(
            flops=12 * degrees * padded * cycles,
            bytes_accessed=2 * orders * degrees * cycles,
            transcendentals=0,
        ),
    )(
        jnp.broadcast_to(cos_row, start_logs.shape),
        start_logs,
        grow[:, :, None],
        (grow * shrink)[:, :, None],
        seed[:, :, None],
    )


def shift_exchange(values, split_axis, concat_axis):
    devices = lax.axis_size("lon")
    place = lax.axis_index("lon")
    split = values.shape[split_axis] // devices
    extent = values.shape[concat_axis]
    shape = list(values.shape)
    shape[split_axis] = split
    shape[concat_axis] = extent * devices
    gathered = jnp.zeros(shape, values.dtype)
    for shift in range(devices):
        target = (place + shift) % devices
        source = (place + devices - shift) % devices
        block = lax.dynamic_slice_in_dim(values, target * split, split, axis=split_axis)
        if shift:
            pairs = [(index, (index + shift) % devices) for index in range(devices)]
            block = lax.ppermute(block, "lon", pairs)
        gathered = lax.dynamic_update_slice_in_dim(
            gathered, block, source * extent, axis=concat_axis
        )
    return gathered


def on_device(grid_state, upstream, spectral_weight, up_weight, down_weight):
    lat_devices = lax.axis_size("lat")
    lon_devices = lax.axis_size("lon")
    lat_rows, lon_cells, channels = grid_state.shape
    degrees = lat_rows * lat_devices
    if lat_rows % lon_devices or (degrees // (lat_devices * lon_devices)) % 4:
        return general_device(grid_state, upstream, spectral_weight, up_weight, down_weight)
    devices = lat_devices * lon_devices
    orders = degrees // devices
    cycles = lat_rows // lon_devices
    lon_total = lon_cells * lon_devices
    both = ("lat", "lon")
    place = lax.axis_index("lat") * lon_devices + lax.axis_index("lon")

    forward_np, inverse_np = fourier_tables(lon_total, order_slots(degrees))

    def by_order(table):
        table = table.reshape(lon_total, 2, devices, orders).transpose(0, 2, 1, 3)
        return jnp.asarray(table.reshape(lon_total, 2 * degrees), jnp.float32).astype(jnp.bfloat16)

    fourier_fwd = by_order(forward_np)
    fourier_inv = by_order(inverse_np.transpose(2, 0, 1))
    cosines, log_sines, quad = latitude_tables(degrees)
    quad_all = jnp.asarray(quad, jnp.float32)
    quad_own = lax.dynamic_slice_in_dim(quad_all, place * cycles, cycles, axis=0)
    order_ids = place * orders + jnp.arange(orders, dtype=jnp.int32)
    table = order_table(order_ids, degrees, cosines, log_sines)
    weight = lax.all_gather(spectral_weight, "lon", axis=0, tiled=True)

    def grid_to_degrees(circles, fourier, scale, waiting):
        spectrum = jnp.einsum("jnc,nq->jqc", circles, fourier, preferred_element_type=jnp.float32)
        if scale is not None:
            spectrum = spectrum * scale[:, None, None]
        spectrum = lax.all_to_all(
            spectrum.astype(jnp.bfloat16), both, split_axis=1, concat_axis=0, tiled=True
        )
        spectrum, waiting = lax.optimization_barrier((spectrum, waiting))
        spectrum = spectrum.reshape(degrees, 2, orders, channels)
        coeffs = jnp.einsum(
            "mlj,jrmc->lrmc", table, spectrum, preferred_element_type=jnp.float32
        ).astype(jnp.bfloat16)
        coeffs = lax.all_to_all(
            coeffs.reshape(lat_devices, lat_rows, 2 * orders, channels), "lat", 0, 0, tiled=True
        ).reshape(lat_devices, lat_rows, 2, orders, channels)
        coeffs = coeffs.transpose(1, 2, 0, 3, 4).reshape(
            lat_rows, 2, lat_devices * orders, channels
        )
        return (coeffs, waiting)

    def degrees_to_grid(coeffs, fourier, scale):
        coeffs = coeffs.reshape(lat_rows, 2, lat_devices, orders, channels).transpose(2, 0, 1, 3, 4)
        coeffs = lax.all_to_all(
            coeffs.reshape(lat_devices, lat_rows, 2 * orders, channels), "lat", 0, 0, tiled=True
        ).reshape(degrees, 2, orders, channels)
        spectrum = jnp.einsum("mlj,lrmc->jrmc", table, coeffs, preferred_element_type=jnp.float32)
        if scale is not None:
            spectrum = spectrum * scale[:, None, None, None]
        spectrum = lax.all_to_all(
            spectrum.astype(jnp.bfloat16).reshape(degrees, 2 * orders, channels),
            both,
            split_axis=0,
            concat_axis=1,
            tiled=True,
        )
        circles = jnp.einsum("jqc,nq->jnc", spectrum, fourier, preferred_element_type=jnp.float32)
        return circles.astype(jnp.bfloat16)

    state = lax.all_to_all(grid_state, "lon", split_axis=0, concat_axis=1, tiled=True)
    coeffs, upstream = grid_to_degrees(state, fourier_fwd, quad_own, upstream)
    upstream = shift_exchange(upstream, 0, 1)
    mixed_coeffs = forward_mix(coeffs, weight).astype(jnp.bfloat16)
    spectral_part = degrees_to_grid(mixed_coeffs, fourier_inv, None)
    mid_state = (state.astype(jnp.float32) + spectral_part.astype(jnp.float32)).astype(
        jnp.bfloat16
    )
    mid_rows = mid_state.reshape(-1, channels)
    hidden = jnp.dot(mid_rows, up_weight, preferred_element_type=jnp.float32)
    act_value, act_pull = jax.vjp(jax.nn.gelu, hidden)
    activation = act_value.astype(jnp.bfloat16)
    next_rows = mid_rows.astype(jnp.float32) + jnp.dot(
        activation, down_weight, preferred_element_type=jnp.float32
    )
    next_state = next_rows.astype(jnp.bfloat16).reshape(cycles, lon_total, channels)
    up_rows = upstream.reshape(-1, channels)
    down_part = jnp.einsum("tf,tc->fc", activation, up_rows, preferred_element_type=jnp.float32)
    pulled = jnp.einsum("tc,fc->tf", up_rows, down_weight, preferred_element_type=jnp.float32)
    grad_hidden = act_pull(pulled)[0].astype(jnp.bfloat16)
    up_part = jnp.einsum("tc,tf->cf", mid_rows, grad_hidden, preferred_element_type=jnp.float32)
    grad_mid = up_rows.astype(jnp.float32) + jnp.einsum(
        "tf,cf->tc", grad_hidden, up_weight, preferred_element_type=jnp.float32
    )
    grad_mid = grad_mid.astype(jnp.bfloat16).reshape(cycles, lon_total, channels)
    grad_mid, up_part, down_part, next_state = lax.optimization_barrier(
        (grad_mid, up_part, down_part, next_state)
    )
    grad_up, grad_down = lax.psum((up_part, down_part), both)
    grad_mixed, next_state = grid_to_degrees(grad_mid, fourier_inv, None, next_state)
    next_state = shift_exchange(next_state, 1, 0)
    grad_mixed, grad_up, grad_down = lax.optimization_barrier((grad_mixed, grad_up, grad_down))
    grad_spectral = lax.psum_scatter(
        weight_grad(coeffs, grad_mixed).astype(jnp.bfloat16), "lon", scatter_dimension=0, tiled=True
    ).astype(jnp.float32)
    grad_coeffs = back_mix(grad_mixed, weight).astype(jnp.bfloat16)
    grad_spectral_part = degrees_to_grid(grad_coeffs, fourier_fwd, quad_all)
    grad_state = (grad_mid.astype(jnp.float32) + grad_spectral_part.astype(jnp.float32)).astype(
        jnp.bfloat16
    )
    grad_state = lax.all_to_all(grad_state, "lon", split_axis=1, concat_axis=0, tiled=True)
    return (next_state, grad_state, grad_spectral, grad_up, grad_down)


def solution(mesh):
    in_specs = (P("lat", "lon", None), P("lat", "lon", None), P("lon", "lat", None, None), P(), P())
    out_specs = (
        P("lat", "lon", None),
        P("lat", "lon", None),
        P("lon", "lat", None, None),
        P(),
        P(),
    )
    return jax.shard_map(
        on_device, mesh=mesh, in_specs=in_specs, out_specs=out_specs, check_vma=False
    )
```
